32 devices in a mesh: tm: 8 (over y, x, core), tensor: 4 (over z).
Axes of the slice: x: 2, y: 2, z: 4, core: 2. Of those that a mesh axis runs over, the one named last changes fastest.
Arguments:
- inputs: bfloat16 [131072, 1536], P('tm', 'tensor'), may hold values from -6 to 6
- kernel: bfloat16 [131072, 1536], P('tm', 'tensor'), may hold values from -5 to 5
- w_in: bfloat16 [12, 128, 128], P('tensor'), may hold values from -0.5 to 0.5
- w_gate: bfloat16 [12, 128, 128], P('tensor'), may hold values from -0.5 to 0.5
- w_out: bfloat16 [12, 128, 128], P('tensor'), may hold values from -0.5 to 0.5
- factor_a: bfloat16 [512, 512], replicated, may hold values from -0.25 to 0.25
- factor_b: bfloat16 [256, 256], replicated, may hold values from -0.375 to 0.375
- cotangent: bfloat16 [131072, 1536], P('tm', 'tensor'), may hold values from -6 to 6
Outputs:
- outputs: bfloat16 [131072, 1536], P('tm', 'tensor')
- grad_inputs: bfloat16 [131072, 1536], P('tm', 'tensor')
- grad_kernel: bfloat16 [131072, 1536], P('tm', 'tensor')
- grad_w_in: float32 [12, 128, 128], P('tensor')
- grad_w_gate: float32 [12, 128, 128], P('tensor')
- grad_w_out: float32 [12, 128, 128], P('tensor')
- grad_factor_a: float32 [512, 512], P('tm')
- grad_factor_b: float32 [256, 256], P('tm')
The draws below stay inside these ranges and needn't reach their ends.
All inputs are finite; a program needn't handle non-finite values.
Results may differ from the reference program's by a relative error of at most 0.0071.
Values may be sent and summed in bfloat16 or wider, within the bound.
No kernel may reach another device: no remote copies, remote signals or barrier semaphores. Data moves between devices by JAX's collectives and lax.ppermute only.
A program may use at most 320 MiB of HBM per device.

```python
import math
import jax
import jax.numpy as jnp

D = 1536
BLOCK = 128
N1 = 256
N2 = 512
LENGTH = 131072
NBLOCKS = 12


def steps_of(rng, extent, cuts, smallest, top_value):
    def one(dim, shards_of):
        heights = jax.random.uniform(jax.random.fold_in(jax.random.fold_in(rng, 6), dim), (shards_of,), jnp.float32, smallest / len(cuts), top_value / len(cuts))
        return jnp.repeat(jnp.exp(heights), extent[dim] // shards_of).reshape((-1,) + (1,) * (len(extent) - dim - 1))

    level = one(*cuts[0])
    for cut in cuts[1:]:
        level = level * one(*cut)
    return level


def gaussian(key, dims, spread, limit, cuts=(), dtype=jnp.bfloat16):
    values = spread * jax.random.normal(key, dims, jnp.float32)
    if cuts:
        values = values * steps_of(key, dims, cuts, -0.22, 0.18)
    return jnp.clip(values, -limit, limit).astype(dtype)


def setup_inputs(seed: int = 0) -> dict:
    key_of = jax.random.split(jax.random.key(seed), 9)
    inputs = gaussian(key_of[0], (LENGTH, D), 1.0, 6.0, ((0, 8), (1, 4)))
    kernel = gaussian(key_of[1], (LENGTH, D), 1.0, 5.0, ((0, 8), (1, 4)))
    w_in = gaussian(key_of[2], (NBLOCKS, BLOCK, BLOCK), BLOCK ** -0.5, 0.5, ((0, 4),))
    w_gate = gaussian(key_of[3], (NBLOCKS, BLOCK, BLOCK), BLOCK ** -0.5, 0.5, ((0, 4),))
    w_out = gaussian(key_of[4], (NBLOCKS, BLOCK, BLOCK), BLOCK ** -0.5, 0.5, ((0, 4),))
    factor_a = gaussian(key_of[5], (N2, N2), N2 ** -0.5, 0.25)
    factor_b = gaussian(key_of[6], (N1, N1), N1 ** -0.5, 0.375)
    cotangent = gaussian(key_of[7], (LENGTH, D), 1.0, 6.0, ((0, 8), (1, 4)))
    return {"inputs": inputs, "kernel": kernel, "w_in": w_in, "w_gate": w_gate, "w_out": w_out, "factor_a": factor_a, "factor_b": factor_b, "cotangent": cotangent}


def mix(act, weight):
    blocks = act.reshape(act.shape[0], D // BLOCK, BLOCK).astype(jnp.float32)
    out = jnp.einsum('tnb,nbe->tne', blocks, weight.astype(jnp.float32))
    return out.reshape(act.shape[0], D)

def mix_back(grad, weight):
    blocks = grad.reshape(grad.shape[0], D // BLOCK, BLOCK).astype(jnp.float32)
    out = jnp.einsum('tne,nbe->tnb', blocks, weight.astype(jnp.float32))
    return out.reshape(grad.shape[0], D)

def mix_grad(act, grad):
    left = act.reshape(act.shape[0], D // BLOCK, BLOCK).astype(jnp.float32)
    right = grad.reshape(grad.shape[0], D // BLOCK, BLOCK).astype(jnp.float32)
    return jnp.einsum('tnb,tne->nbe', left, right) / math.sqrt(N1 * N2)

def reference(inputs, kernel, w_in, w_gate, w_out, factor_a, factor_b, cotangent):
    fa = factor_a.astype(jnp.float32)
    fb = factor_b.astype(jnp.float32)
    mixed_in = mix(inputs, w_in).astype(jnp.bfloat16)
    gate = mix(inputs, w_gate)
    mixed3 = mixed_in.reshape(N1, N2, D)
    first = jnp.einsum('ijc,jk->ikc', mixed3.astype(jnp.float32), fa)
    twiddle = kernel.reshape(N1, N2, D).astype(jnp.float32)
    twisted = (first * twiddle).astype(jnp.bfloat16)
    second = jnp.einsum('im,ikc->mkc', fb, twisted.astype(jnp.float32)).astype(jnp.bfloat16)
    second = second.reshape(N1 * N2, D)
    gated = (second.astype(jnp.float32) * gate).astype(jnp.bfloat16)
    outputs = mix(gated, w_out).astype(jnp.bfloat16)
    grad_gated = mix_back(cotangent, w_out)
    grad_second = (grad_gated * gate).astype(jnp.bfloat16)
    grad_gate = (grad_gated * second.astype(jnp.float32)).astype(jnp.bfloat16)
    grad_second3 = grad_second.reshape(N1, N2, D).astype(jnp.float32)
    grad_twisted = jnp.einsum('im,mkc->ikc', fb, grad_second3).astype(jnp.bfloat16)
    grad_factor_b = jnp.einsum('ikc,mkc->im', twisted.astype(jnp.float32), grad_second3) / math.sqrt(N2 * D)
    grad_tw32 = grad_twisted.astype(jnp.float32)
    grad_first = (grad_tw32 * twiddle).astype(jnp.bfloat16)
    grad_kernel = (grad_tw32 * first).astype(jnp.bfloat16).reshape(N1 * N2, D)
    grad_first32 = grad_first.astype(jnp.float32)
    grad_factor_a = jnp.einsum('ijc,ikc->jk', mixed3.astype(jnp.float32), grad_first32) / math.sqrt(N1 * D)
    grad_mixed = jnp.einsum('jk,ikc->ijc', fa, grad_first32).astype(jnp.bfloat16).reshape(N1 * N2, D)
    grad_inputs = (mix_back(grad_mixed, w_in) + mix_back(grad_gate, w_gate)).astype(jnp.bfloat16)
    grad_w_in = mix_grad(inputs, grad_mixed)
    grad_w_gate = mix_grad(inputs, grad_gate)
    grad_w_out = mix_grad(gated, cotangent)
    return (outputs, grad_inputs, grad_kernel, grad_w_in, grad_w_gate, grad_w_out, grad_factor_a, grad_factor_b)
```

```python
import functools
import math

import jax
import jax.numpy as jnp
from jax import lax
from jax.experimental import pallas as pl
from jax.experimental.pallas import tpu as pltpu
from jax.sharding import PartitionSpec as P

D = 1536
N1 = 256
N2 = 512
BF = jnp.bfloat16
F32 = jnp.float32
VMEM_LIMIT = 56 * 1024 * 1024


def dot(left, right):
    return jnp.dot(left, right, preferred_element_type=F32)


def dot_nt(left, right):
    return lax.dot_general(left, right, (((1,), (1,)), ((), ())), preferred_element_type=F32)


def dot_tn(left, right):
    return lax.dot_general(left, right, (((0,), (0,)), ((), ())), preferred_element_type=F32)


def params(dims):
    return pltpu.CompilerParams(
        dimension_semantics=("arbitrary",) * dims, vmem_limit_bytes=VMEM_LIMIT
    )


def cost(flops, nbytes):
    return pl.CostEstimate(flops=int(flops), bytes_accessed=int(nbytes), transcendentals=0)


def stack_rows(pieces):
    if pieces[0].shape[0] % 16 == 0:
        return jnp.concatenate(pieces, axis=0)
    return jnp.concatenate([p.astype(F32) for p in pieces], axis=0).astype(BF)


def grad_second_kernel(p_ref, x_ref, ct_ref, wg_ref, wo_ref, out_ref, scr):
    blocks, span, width = x_ref.shape
    x = x_ref[...].reshape(blocks * span, width)
    ct = ct_ref[...].reshape(blocks * span, width)
    scr[...] = dot_nt(ct, wo_ref[0]) * dot(x, wg_ref[0])
    for k in range(span):
        out_ref[k] = scr[pl.ds(k, blocks, stride=span), :].astype(BF)


def grad_second_call(partner, x3, ct3, w_gate, w_out, span):
    blocks, inner, chans = x3.shape
    width = w_gate.shape[1]
    rows = pl.BlockSpec((blocks, span, width), lambda n, p: (0, p[0], n))
    weight = pl.BlockSpec((1, width, width), lambda n, p: (n, 0, 0))
    size = blocks * span * chans
    return pl.pallas_call(
        grad_second_kernel,
        grid_spec=pltpu.PrefetchScalarGridSpec(
            num_scalar_prefetch=1,
            grid=(chans // width,),
            in_specs=[rows, rows, weight, weight],
            out_specs=pl.BlockSpec((span, blocks, width), lambda n, p: (0, 0, n)),
            scratch_shapes=[pltpu.VMEM((blocks * span, width), F32)],
        ),
        out_shape=jax.ShapeDtypeStruct((span, blocks, chans), BF),
        compiler_params=params(1),
        cost_estimate=cost(4 * size * width, 6 * size),
        name="grad_second",
    )(partner, x3, ct3, w_gate, w_out)


def twisted_kernel(me_ref, x_ref, kn_ref, wi_ref, at_ref, *rest):
    outs, scr = rest[:-1], rest[-1]
    some, inner, width = x_ref.shape
    span, blocks, _ = outs[0].shape
    step = pl.program_id(1)
    mixed = dot(x_ref[...].reshape(some * inner, width), wi_ref[0]).astype(BF)
    for q in range(0, some, 2):
        pair = jnp.concatenate(
            [mixed[q * inner : (q + 1) * inner], mixed[(q + 1) * inner : (q + 2) * inner]], axis=1
        )
        first = dot(at_ref[...], pair)
        for h in range(2):
            value = first[:, h * width : (h + 1) * width] * kn_ref[q + h].astype(F32)
            scr[pl.ds(step * some + q + h, inner, stride=blocks), :] = value

    @pl.when(step == pl.num_programs(1) - 1)
    def _():
        for d, out in enumerate(outs):
            first_row = pl.multiple_of((me_ref[0] ^ d) * (span * blocks), span * blocks)
            piece = scr[pl.ds(first_row, span * blocks), :]
            out[...] = piece.reshape(span, blocks, width).astype(BF)


def twisted_call(me, x3, kn3, w_in, factor_at, parts):
    blocks, inner, chans = x3.shape
    width = w_in.shape[1]
    span = inner // parts
    some = 4
    rows = pl.BlockSpec((some, inner, width), lambda n, i, m: (i, 0, n))
    out = pl.BlockSpec((span, blocks, width), lambda n, i, m: (0, 0, n))
    size = blocks * inner * chans
    return pl.pallas_call(
        twisted_kernel,
        grid_spec=pltpu.PrefetchScalarGridSpec(
            num_scalar_prefetch=1,
            grid=(chans // width, blocks // some),
            in_specs=[
                rows,
                rows,
                pl.BlockSpec((1, width, width), lambda n, i, m: (n, 0, 0)),
                pl.BlockSpec((inner, inner), lambda n, i, m: (0, 0)),
            ],
            out_specs=[out] * parts,
            scratch_shapes=[pltpu.VMEM((inner * blocks, width), F32)],
        ),
        out_shape=[jax.ShapeDtypeStruct((span, blocks, chans), BF)] * parts,
        compiler_params=params(2),
        cost_estimate=cost(2 * size * (width + inner), 6 * size),
        name="twisted",
    )(me, x3, kn3, w_in, factor_at)


def grad_twisted_kernel(fb_ref, *refs):
    parts = len(refs) // 2
    ins, outs = refs[:parts], refs[parts:]
    some, blocks, _ = ins[0].shape
    for k in range(some):
        value = dot(fb_ref[...], stack_rows([ref[k] for ref in ins])).astype(BF)
        for d in range(parts):
            outs[d][k] = value[d * blocks : (d + 1) * blocks]


def grad_twisted_call(fb, arrays):
    parts = len(arrays)
    span, blocks, chans = arrays[0].shape
    some = 8
    spec = pl.BlockSpec((some, blocks, chans), lambda k: (k, 0, 0))
    size = parts * span * blocks * chans
    return pl.pallas_call(
        grad_twisted_kernel,
        grid=(span // some,),
        in_specs=[pl.BlockSpec(fb.shape, lambda k: (0, 0))] + [spec] * parts,
        out_specs=[spec] * parts,
        out_shape=[jax.ShapeDtypeStruct((span, blocks, chans), BF)] * parts,
        compiler_params=params(1),
        cost_estimate=cost(2 * size * fb.shape[0], 4 * size),
        name="grad_twisted",
    )(fb, *arrays)


def second_kernel(fbt_ref, *refs):
    parts = (len(refs) - 1) // 3
    tws, gss, outs, fbg = refs[:parts], refs[parts : 2 * parts], refs[2 * parts : -1], refs[-1]
    some, blocks, _ = tws[0].shape

    @pl.when(pl.program_id(0) == 0)
    def _():
        fbg[...] = jnp.zeros_like(fbg)

    for k in range(some):
        tw = stack_rows([ref[k] for ref in tws])
        gs = stack_rows([ref[k] for ref in gss])
        value = dot(fbt_ref[...], tw).astype(BF)
        for d in range(parts):
            outs[d][k] = value[d * blocks : (d + 1) * blocks]
        fbg[...] += dot_nt(tw, gs)


def second_call(fbt, tws, gss):
    parts = len(tws)
    span, blocks, chans = tws[0].shape
    some = 8
    spec = pl.BlockSpec((some, blocks, chans), lambda k: (k, 0, 0))
    whole = pl.BlockSpec(fbt.shape, lambda k: (0, 0))
    size = parts * span * blocks * chans
    result = pl.pallas_call(
        second_kernel,
        grid=(span // some,),
        in_specs=[whole] + [spec] * (2 * parts),
        out_specs=[spec] * parts + [whole],
        out_shape=[jax.ShapeDtypeStruct((span, blocks, chans), BF)] * parts
        + [jax.ShapeDtypeStruct(fbt.shape, F32)],
        compiler_params=params(1),
        cost_estimate=cost(4 * size * fbt.shape[0], 6 * size),
        name="second",
    )(fbt, *tws, *gss)
    return result[:-1], result[-1]


def grad_mixed_kernel(me_ref, x_ref, kn_ref, wi_ref, at_ref, a_ref, *rest):
    gts = rest[:-5]
    gk_ref, gm_ref, fag, gwi, scr = rest[-5:]
    some, inner, width = x_ref.shape
    span, blocks, _ = gts[0].shape
    step = pl.program_id(1)

    @pl.when(step == 0)
    def _():
        gwi[...] = jnp.zeros_like(gwi)
        for d, ref in enumerate(gts):
            first_row = pl.multiple_of((me_ref[0] ^ d) * (span * blocks), span * blocks)
            scr[pl.ds(first_row, span * blocks), :] = (
                ref[...].astype(F32).reshape(span * blocks, width)
            )

    @pl.when((step == 0) & (pl.program_id(0) == 0))
    def _():
        fag[...] = jnp.zeros_like(fag)

    x = x_ref[...].reshape(some * inner, width)
    mixed = dot(x, wi_ref[0]).astype(BF)
    for q in range(0, some, 2):
        pair = jnp.concatenate(
            [mixed[q * inner : (q + 1) * inner], mixed[(q + 1) * inner : (q + 2) * inner]], axis=1
        )
        first = dot(at_ref[...], pair)
        grads = []
        for h in range(2):
            gt = scr[pl.ds(step * some + q + h, inner, stride=blocks), :]
            gk_ref[q + h] = (gt * first[:, h * width : (h + 1) * width]).astype(BF)
            grads.append((gt * kn_ref[q + h].astype(F32)).astype(BF))
        grad_first = jnp.concatenate(grads, axis=1)
        fag[...] += dot_nt(pair, grad_first)
        grad_mixed = dot(a_ref[...], grad_first).astype(BF)
        for h in range(2):
            gm_ref[q + h] = grad_mixed[:, h * width : (h + 1) * width]
    gwi[0] += dot_tn(x, gm_ref[...].reshape(some * inner, width))


def grad_mixed_call(me, x3, kn3, w_in, factor_at, factor_a, gts):
    parts = len(gts)
    blocks, inner, chans = x3.shape
    width = w_in.shape[1]
    span = inner // parts
    some = 4
    rows = pl.BlockSpec((some, inner, width), lambda n, i, m: (i, 0, n))
    weight = pl.BlockSpec((1, width, width), lambda n, i, m: (n, 0, 0))
    whole = pl.BlockSpec((inner, inner), lambda n, i, m: (0, 0))
    size = blocks * inner * chans
    return pl.pallas_call(
        grad_mixed_kernel,
        grid_spec=pltpu.PrefetchScalarGridSpec(
            num_scalar_prefetch=1,
            grid=(chans // width, blocks // some),
            in_specs=[rows, rows, weight, whole, whole]
            + [pl.BlockSpec((span, blocks, width), lambda n, i, m: (0, 0, n))] * parts,
            out_specs=[rows, rows, whole, weight],
            scratch_shapes=[pltpu.VMEM((inner * blocks, width), F32)],
        ),
        out_shape=[
            jax.ShapeDtypeStruct(x3.shape, BF),
            jax.ShapeDtypeStruct(x3.shape, BF),
            jax.ShapeDtypeStruct((inner, inner), F32),
            jax.ShapeDtypeStruct(w_in.shape, F32),
        ],
        compiler_params=params(2),
        cost_estimate=cost(2 * size * (2 * width + 3 * inner), 10 * size),
        name="grad_mixed",
    )(me, x3, kn3, w_in, factor_at, factor_a, *gts)


def outputs_kernel(p_ref, x_ref, ct_ref, gm_ref, se_ref, wi_ref, wg_ref, wo_ref, *rest):
    out_ref, gi_ref, gwg, gwo, scr = rest[-5:]
    before = rest[:-5]
    blocks, span, width = x_ref.shape
    rows = blocks * span
    x = x_ref[...].reshape(rows, width)
    ct = ct_ref[...].reshape(rows, width)
    scr[...] = se_ref[...].astype(F32).reshape(rows, width)
    second = jnp.concatenate(
        [scr[pl.ds(i, span, stride=blocks), :] for i in range(blocks)], axis=0
    )
    gated = (second * dot(x, wg_ref[0])).astype(BF)
    out_ref[...] = dot(gated, wo_ref[0]).astype(BF).reshape(blocks, span, width)
    grad_gate = (dot_nt(ct, wo_ref[0]) * second).astype(BF)
    grad_mixed = gm_ref[...].reshape(rows, width)
    grad_inputs = dot_nt(grad_mixed, wi_ref[0]) + dot_nt(grad_gate, wg_ref[0])
    gi_ref[...] = grad_inputs.astype(BF).reshape(blocks, span, width)
    gate_term = dot_tn(x, grad_gate)
    out_term = dot_tn(gated, ct)
    if before:
        gate_term += before[2][0]
        out_term += before[3][0]
    gwg[0] = gate_term
    gwo[0] = out_term


def outputs_call(partner, x3, ct3, gm3, second, w_in, w_gate, w_out, before):
    blocks, inner, chans = x3.shape
    width = w_in.shape[1]
    span = second.shape[0]
    rows = pl.BlockSpec((blocks, span, width), lambda n, p: (0, p[0], n))
    weight = pl.BlockSpec((1, width, width), lambda n, p: (n, 0, 0))
    anywhere = pl.BlockSpec(memory_space=pl.ANY)
    size = blocks * span * chans
    return pl.pallas_call(
        outputs_kernel,
        grid_spec=pltpu.PrefetchScalarGridSpec(
            num_scalar_prefetch=1,
            grid=(chans // width,),
            in_specs=[
                rows,
                rows,
                rows,
                pl.BlockSpec((span, blocks, width), lambda n, p: (0, 0, n)),
                weight,
                weight,
                weight,
            ]
            + ([anywhere, anywhere, weight, weight] if before else []),
            out_specs=[rows, rows, weight, weight],
            scratch_shapes=[pltpu.VMEM((blocks * span, width), F32)],
        ),
        out_shape=[
            jax.ShapeDtypeStruct(x3.shape, BF),
            jax.ShapeDtypeStruct(x3.shape, BF),
            jax.ShapeDtypeStruct(w_in.shape, F32),
            jax.ShapeDtypeStruct(w_in.shape, F32),
        ],
        input_output_aliases={8: 0, 9: 1} if before else {},
        compiler_params=params(1),
        cost_estimate=cost(14 * size * width, 12 * size),
        name="outputs",
    )(partner, x3, ct3, gm3, second, w_in, w_gate, w_out, *before)


def exchange(array, d, parts):
    if d == 0:
        return array
    return lax.ppermute(array, "tm", [(i, i ^ d) for i in range(parts)])


def send_order(parts):
    return list(range(parts - 1, -1, -1))


def body(parts, inputs, kernel, w_in, w_gate, w_out, factor_a, factor_b, cotangent):
    rows, chans = inputs.shape
    inner = factor_a.shape[0]
    blocks = rows // inner
    span = inner // parts
    me = lax.axis_index("tm").astype(jnp.int32)
    me1 = me[None]
    partners = me ^ jnp.arange(parts, dtype=jnp.int32)
    x3 = inputs.reshape(blocks, inner, chans)
    kn3 = kernel.reshape(blocks, inner, chans)
    ct3 = cotangent.reshape(blocks, inner, chans)
    factor_at = factor_a.T
    order = send_order(parts)

    spread = (partners[:, None] * blocks + jnp.arange(blocks, dtype=jnp.int32)).reshape(-1)
    fb = jnp.take(jnp.take(factor_b, spread, axis=0), spread, axis=1)

    gs_in = [None] * parts
    for d in order:
        piece = grad_second_call(partners[d][None], x3, ct3, w_gate, w_out, span)
        gs_in[d] = exchange(piece, d, parts)
    tw_out = twisted_call(me1, x3, kn3, w_in, factor_at, parts)
    tw_in = [None] * parts
    for d in order:
        tw_in[d] = exchange(tw_out[d], d, parts)
    gt_out = grad_twisted_call(fb, gs_in)
    gt_in = [None] * parts
    for d in order:
        gt_in[d] = exchange(gt_out[d], d, parts)
    se_out, fb_term = second_call(fb.T, tw_in, gs_in)
    se_in = [None] * parts
    for d in order:
        se_in[d] = exchange(se_out[d], d, parts)
    gk, gm, fa_term, gwi_term = grad_mixed_call(
        me1, x3, kn3, w_in, factor_at, factor_a, gt_in
    )
    state = ()
    for d in order[-1:] + order[:-1]:
        state = outputs_call(
            partners[d][None], x3, ct3, gm, se_in[d], w_in, w_gate, w_out, state
        )
    outputs, grad_inputs, gwg_term, gwo_term = state

    fb_term = jnp.take(jnp.take(fb_term, spread, axis=0), spread, axis=1)
    token_scale = 1.0 / math.sqrt(N1 * N2)
    fa_piece = lax.psum_scatter(fa_term, "tm", scatter_dimension=0, tiled=True)
    fb_piece = lax.psum_scatter(fb_term, "tm", scatter_dimension=0, tiled=True)
    grad_factor_a = lax.psum(fa_piece, "tensor") / math.sqrt(N1 * D)
    grad_factor_b = lax.psum(fb_piece, "tensor") / math.sqrt(N2 * D)
    summed_in = lax.psum(gwi_term, "tm")
    summed_gate, summed_out = lax.psum((gwg_term, gwo_term), "tm")
    return (
        outputs.reshape(rows, chans),
        grad_inputs.reshape(rows, chans),
        gk.reshape(rows, chans),
        summed_in * token_scale,
        summed_gate * token_scale,
        summed_out * token_scale,
        grad_factor_a,
        grad_factor_b,
    )


def solution(mesh):
    return jax.shard_map(
        functools.partial(body, mesh.shape["tm"]),
        mesh=mesh,
        in_specs=(
            P("tm", "tensor"),
            P("tm", "tensor"),
            P("tensor", None, None),
            P("tensor", None, None),
            P("tensor", None, None),
            P(),
            P(),
            P("tm", "tensor"),
        ),
        out_specs=(
            P("tm", "tensor"),
            P("tm", "tensor"),
            P("tm", "tensor"),
            P("tensor", None, None),
            P("tensor", None, None),
            P("tensor", None, None),
            P("tm", None),
            P("tm", None),
        ),
        check_vma=False,
    )
```

```python
import functools
import math

import jax
import jax.numpy as jnp
from jax import lax
from jax.experimental import pallas as pl
from jax.experimental.pallas import tpu as pltpu
from jax.sharding import PartitionSpec as P

D = 1536
N1 = 256
N2 = 512
BF = jnp.bfloat16
F32 = jnp.float32
VMEM_LIMIT = 56 * 1024 * 1024
COST = 0.1


def dot(left, right):
    return jnp.dot(left, right, preferred_element_type=F32)


def dot_nt(left, right):
    return lax.dot_general(left, right, (((1,), (1,)), ((), ())), preferred_element_type=F32)


def dot_tn(left, right):
    return lax.dot_general(left, right, (((0,), (0,)), ((), ())), preferred_element_type=F32)


def diagonal(first, second):
    zero = jnp.zeros_like(first)
    return jnp.concatenate(
        [jnp.concatenate([first, zero], axis=1), jnp.concatenate([zero, second], axis=1)], axis=0
    )


def params(dims):
    return pltpu.CompilerParams(
        dimension_semantics=("arbitrary",) * dims, vmem_limit_bytes=VMEM_LIMIT
    )


def cost(flops, nbytes):
    return pl.CostEstimate(flops=int(flops * COST), bytes_accessed=int(nbytes * COST), transcendentals=0)


def stack_rows(pieces):
    if pieces[0].shape[0] % 16 == 0:
        return jnp.concatenate(pieces, axis=0)
    return jnp.concatenate([p.astype(F32) for p in pieces], axis=0).astype(BF)


def grad_second_kernel(p_ref, x_ref, ct_ref, wg_ref, wo_ref, *rest):
    out_ref = rest[-1]
    blocks, span, chans = x_ref.shape
    width = wg_ref.shape[1]
    rows = blocks * span
    for n in range(chans // width):
        lanes = slice(n * width, (n + 1) * width)
        x = x_ref[:, :, lanes].reshape(rows, width)
        ct = ct_ref[:, :, lanes].reshape(rows, width)
        both = dot(jnp.concatenate([x, ct], axis=1), diagonal(wg_ref[n], wo_ref[n].T))
        value = (both[:, :width] * both[:, width:]).astype(BF)
        out_ref[:, :, lanes] = jnp.swapaxes(value.reshape(blocks, span, width), 0, 1)


def grad_second_call(partner, x3, ct3, w_gate, w_out, span, after):
    blocks, inner, chans = x3.shape
    width = w_gate.shape[1]
    some = min(blocks, 16)
    rows = pl.BlockSpec((some, span, chans), lambda i, p: (i, p[0], 0))
    weight = pl.BlockSpec(w_gate.shape, lambda i, p: (0, 0, 0))
    anywhere = pl.BlockSpec(memory_space=pl.ANY)
    size = blocks * span * chans
    return pl.pallas_call(
        grad_second_kernel,
        grid_spec=pltpu.PrefetchScalarGridSpec(
            num_scalar_prefetch=1,
            grid=(blocks // some,),
            in_specs=[rows, rows, weight, weight] + [anywhere] * len(after),
            out_specs=pl.BlockSpec((span, some, chans), lambda i, p: (0, i, 0)),
        ),
        out_shape=jax.ShapeDtypeStruct((span, blocks, chans), BF),
        compiler_params=params(1),
        cost_estimate=cost(4 * size * width, 6 * size),
        name="grad_second",
    )(partner, x3, ct3, w_gate, w_out, *after)


def twisted_kernel(dist, me_ref, x_ref, kn_ref, wi_ref, at_ref, *rest):
    some, inner, width = x_ref.shape
    scr = rest[-1]
    blocks = scr.shape[0] // inner
    outs = rest[-1 - len(dist) : -1]
    span = inner // len(dist)
    step = pl.program_id(1)
    mixed = dot(x_ref[...].reshape(some * inner, width), wi_ref[0]).astype(BF)
    for q in range(0, some, 2):
        pair = jnp.concatenate(
            [mixed[q * inner : (q + 1) * inner], mixed[(q + 1) * inner : (q + 2) * inner]], axis=1
        )
        first = dot(at_ref[...], pair)
        for h in range(2):
            value = first[:, h * width : (h + 1) * width] * kn_ref[q + h].astype(F32)
            scr[pl.ds(step * some + q + h, inner, stride=blocks), :] = value

    @pl.when(step == pl.num_programs(1) - 1)
    def _():
        for d, out in zip(dist, outs):
            first_row = pl.multiple_of((me_ref[0] ^ d) * (span * blocks), span * blocks)
            piece = scr[pl.ds(first_row, span * blocks), :]
            out[...] = piece.reshape(span, blocks, width).astype(BF)


def twisted_call(me, x3, kn3, w_in, factor_at, dist, after):
    parts = len(dist)
    blocks, inner, chans = x3.shape
    width = w_in.shape[1]
    span = inner // parts
    some = 4
    rows = pl.BlockSpec((some, inner, width), lambda n, i, m: (i, 0, n))
    out = pl.BlockSpec((span, blocks, width), lambda n, i, m: (0, 0, n))
    size = blocks * inner * chans
    return pl.pallas_call(
        functools.partial(twisted_kernel, dist),
        grid_spec=pltpu.PrefetchScalarGridSpec(
            num_scalar_prefetch=1,
            grid=(chans // width, blocks // some),
            in_specs=[
                rows,
                rows,
                pl.BlockSpec((1, width, width), lambda n, i, m: (n, 0, 0)),
                pl.BlockSpec((inner, inner), lambda n, i, m: (0, 0)),
            ]
            + [pl.BlockSpec(memory_space=pl.ANY)] * len(after),
            out_specs=[out] * parts,
            scratch_shapes=[pltpu.VMEM((inner * blocks, width), F32)],
        ),
        out_shape=[jax.ShapeDtypeStruct((span, blocks, chans), BF)] * parts,
        compiler_params=params(2),
        cost_estimate=cost(2 * size * (width + inner), 6 * size),
        name="twisted",
    )(me, x3, kn3, w_in, factor_at, *after)


def grad_twisted_kernel(fb_ref, *refs):
    parts = len(refs) // 2
    ins, outs = refs[:parts], refs[parts:]
    some, blocks, _ = ins[0].shape
    for k in range(some):
        value = dot(fb_ref[...], stack_rows([ref[k] for ref in ins])).astype(BF)
        for d in range(parts):
            outs[d][k] = value[d * blocks : (d + 1) * blocks]


def grad_twisted_call(fb, arrays):
    parts = len(arrays)
    span, blocks, chans = arrays[0].shape
    some = 8
    spec = pl.BlockSpec((some, blocks, chans), lambda k: (k, 0, 0))
    size = parts * span * blocks * chans
    return pl.pallas_call(
        grad_twisted_kernel,
        grid=(span // some,),
        in_specs=[pl.BlockSpec(fb.shape, lambda k: (0, 0))] + [spec] * parts,
        out_specs=[spec] * parts,
        out_shape=[jax.ShapeDtypeStruct((span, blocks, chans), BF)] * parts,
        compiler_params=params(1),
        cost_estimate=cost(2 * size * fb.shape[0], 4 * size),
        name="grad_twisted",
    )(fb, *arrays)


def second_kernel(fbt_ref, *refs):
    parts = (len(refs) - 1) // 3
    tws, gss, outs, fbg = refs[:parts], refs[parts : 2 * parts], refs[2 * parts : -1], refs[-1]
    some, blocks, _ = tws[0].shape

    @pl.when(pl.program_id(0) == 0)
    def _():
        fbg[...] = jnp.zeros_like(fbg)

    for k in range(some):
        tw = stack_rows([ref[k] for ref in tws])
        gs = stack_rows([ref[k] for ref in gss])
        value = dot(fbt_ref[...], tw).astype(BF)
        for d in range(parts):
            outs[d][k] = value[d * blocks : (d + 1) * blocks]
        fbg[...] += dot_nt(tw, gs)


def second_call(fbt, tws, gss):
    parts = len(tws)
    span, blocks, chans = tws[0].shape
    some = 8
    spec = pl.BlockSpec((some, blocks, chans), lambda k: (k, 0, 0))
    whole = pl.BlockSpec(fbt.shape, lambda k: (0, 0))
    size = parts * span * blocks * chans
    result = pl.pallas_call(
        second_kernel,
        grid=(span // some,),
        in_specs=[whole] + [spec] * (2 * parts),
        out_specs=[spec] * parts + [whole],
        out_shape=[jax.ShapeDtypeStruct((span, blocks, chans), BF)] * parts
        + [jax.ShapeDtypeStruct(fbt.shape, F32)],
        compiler_params=params(1),
        cost_estimate=cost(4 * size * fbt.shape[0], 6 * size),
        name="second",
    )(fbt, *tws, *gss)
    return result[:-1], result[-1]


def grad_mixed_kernel(dist, me_ref, x_ref, kn_ref, wi_ref, at_ref, a_ref, *rest):
    gts = rest[:-5]
    gk_ref, gm_ref, fag, gwi, scr = rest[-5:]
    some, inner, width = x_ref.shape
    span, blocks, _ = gts[0].shape
    step = pl.program_id(1)

    @pl.when(step == 0)
    def _():
        gwi[...] = jnp.zeros_like(gwi)
        for d, ref in zip(dist, gts):
            first_row = pl.multiple_of((me_ref[0] ^ d) * (span * blocks), span * blocks)
            scr[pl.ds(first_row, span * blocks), :] = (
                ref[...].astype(F32).reshape(span * blocks, width)
            )

    @pl.when((step == 0) & (pl.program_id(0) == 0))
    def _():
        fag[...] = jnp.zeros_like(fag)

    x = x_ref[...].reshape(some * inner, width)
    mixed = dot(x, wi_ref[0]).astype(BF)
    for q in range(0, some, 2):
        pair = jnp.concatenate(
            [mixed[q * inner : (q + 1) * inner], mixed[(q + 1) * inner : (q + 2) * inner]], axis=1
        )
        first = dot(at_ref[...], pair)
        grads = []
        for h in range(2):
            gt = scr[pl.ds(step * some + q + h, inner, stride=blocks), :]
            gk_ref[q + h] = (gt * first[:, h * width : (h + 1) * width]).astype(BF)
            grads.append((gt * kn_ref[q + h].astype(F32)).astype(BF))
        grad_first = jnp.concatenate(grads, axis=1)
        fag[...] += dot_nt(pair, grad_first)
        grad_mixed = dot(a_ref[...], grad_first).astype(BF)
        for h in range(2):
            gm_ref[q + h] = grad_mixed[:, h * width : (h + 1) * width]
    gwi[0] += dot_tn(x, gm_ref[...].reshape(some * inner, width))


def grad_mixed_call(me, x3, kn3, w_in, factor_at, factor_a, dist, gts):
    parts = len(gts)
    blocks, inner, chans = x3.shape
    width = w_in.shape[1]
    span = inner // parts
    some = 4
    rows = pl.BlockSpec((some, inner, width), lambda n, i, m: (i, 0, n))
    weight = pl.BlockSpec((1, width, width), lambda n, i, m: (n, 0, 0))
    whole = pl.BlockSpec((inner, inner), lambda n, i, m: (0, 0))
    size = blocks * inner * chans
    return pl.pallas_call(
        functools.partial(grad_mixed_kernel, dist),
        grid_spec=pltpu.PrefetchScalarGridSpec(
            num_scalar_prefetch=1,
            grid=(chans // width, blocks // some),
            in_specs=[rows, rows, weight, whole, whole]
            + [pl.BlockSpec((span, blocks, width), lambda n, i, m: (0, 0, n))] * parts,
            out_specs=[rows, rows, whole, weight],
            scratch_shapes=[pltpu.VMEM((inner * blocks, width), F32)],
        ),
        out_shape=[
            jax.ShapeDtypeStruct(x3.shape, BF),
            jax.ShapeDtypeStruct(x3.shape, BF),
            jax.ShapeDtypeStruct((inner, inner), F32),
            jax.ShapeDtypeStruct(w_in.shape, F32),
        ],
        compiler_params=params(2),
        cost_estimate=cost(2 * size * (2 * width + 3 * inner), 10 * size),
        name="grad_mixed",
    )(me, x3, kn3, w_in, factor_at, factor_a, *gts)


def outputs_kernel(p_ref, x_ref, ct_ref, gm_ref, se_ref, wi_ref, wg_ref, wo_ref, *rest):
    out_ref, gi_ref, gw = rest[-3:]
    before = rest[:-3]
    mixers = wi_ref.shape[0]
    blocks, span, chans = x_ref.shape
    width = wi_ref.shape[1]
    rows = blocks * span

    @pl.when(pl.program_id(0) == 0)
    def _():
        gw[...] = before[2][...] if before else jnp.zeros_like(gw)

    for n in range(chans // width):
        lanes = slice(n * width, (n + 1) * width)
        x = x_ref[:, :, lanes].reshape(rows, width)
        ct = ct_ref[:, :, lanes].reshape(rows, width)
        second = jnp.swapaxes(se_ref[:, :, lanes], 0, 1).astype(F32).reshape(rows, width)
        both = dot(jnp.concatenate([x, ct], axis=1), diagonal(wg_ref[n], wo_ref[n].T))
        gated = (second * both[:, :width]).astype(BF)
        grad_gate = (both[:, width:] * second).astype(BF)
        out_ref[:, :, lanes] = dot(gated, wo_ref[n]).astype(BF).reshape(blocks, span, width)
        grads = jnp.concatenate([gm_ref[:, :, lanes].reshape(rows, width), grad_gate], axis=1)
        back = jnp.concatenate([wi_ref[n].T, wg_ref[n].T], axis=0)
        gi_ref[:, :, lanes] = dot(grads, back).astype(BF).reshape(blocks, span, width)
        terms = dot_tn(
            jnp.concatenate([x, gated], axis=1), jnp.concatenate([grad_gate, ct], axis=1)
        )
        gw[n] += terms[:width, :width]
        gw[mixers + n] += terms[width:, width:]


def outputs_call(partner, x3, ct3, gm3, second, w_in, w_gate, w_out, before):
    blocks, inner, chans = x3.shape
    width = w_in.shape[1]
    span = second.shape[0]
    some = min(blocks, 16)
    rows = pl.BlockSpec((some, span, chans), lambda i, p: (i, p[0], 0))
    weight = pl.BlockSpec(w_in.shape, lambda i, p: (0, 0, 0))
    both = (2 * w_in.shape[0], width, width)
    grads = pl.BlockSpec(both, lambda i, p: (0, 0, 0))
    anywhere = pl.BlockSpec(memory_space=pl.ANY)
    size = blocks * span * chans
    return pl.pallas_call(
        outputs_kernel,
        grid_spec=pltpu.PrefetchScalarGridSpec(
            num_scalar_prefetch=1,
            grid=(blocks // some,),
            in_specs=[
                rows,
                rows,
                rows,
                pl.BlockSpec((span, some, chans), lambda i, p: (0, i, 0)),
                weight,
                weight,
                weight,
            ]
            + ([anywhere, anywhere, grads] if before else []),
            out_specs=[rows, rows, grads],
        ),
        out_shape=[
            jax.ShapeDtypeStruct(x3.shape, BF),
            jax.ShapeDtypeStruct(x3.shape, BF),
            jax.ShapeDtypeStruct(both, F32),
        ],
        input_output_aliases={8: 0, 9: 1} if before else {},
        compiler_params=params(1),
        cost_estimate=cost(14 * size * width, 12 * size),
        name="outputs",
    )(partner, x3, ct3, gm3, second, w_in, w_gate, w_out, *before)


def nothing_kernel(*refs):
    pass


def wait_for(arrays, after):
    anywhere = pl.BlockSpec(memory_space=pl.ANY)
    return pl.pallas_call(
        nothing_kernel,
        in_specs=[anywhere] * (len(arrays) + len(after)),
        out_specs=[anywhere] * len(arrays),
        out_shape=[jax.ShapeDtypeStruct(a.shape, a.dtype) for a in arrays],
        input_output_aliases={i: i for i in range(len(arrays))},
        compiler_params=pltpu.CompilerParams(vmem_limit_bytes=VMEM_LIMIT),
        name="wait_for",
    )(*arrays, *after)


def permute(array, d, parts, axis="tm"):
    return lax.ppermute(array, axis, [(i, i ^ d) for i in range(parts)])


def distances(parts):
    far = sorted(range(2, parts), key=lambda d: (-bin(d >> 1).count("1"), -(d & 1), -d))
    return [0] + far[:2] + [1] + far[2:]


def send(dist, arrays, received, window, parts):
    into = [arrays[0]]
    for d, array in zip(dist[1:], arrays[1:]):
        if len(received) >= window:
            (array,) = wait_for([array], [received[-window]])
        received.append(permute(array, d, parts))
        into.append(received[-1])
    return into


def sum_terms(pieces, whole, me, parts, tensors, after, last):
    chips = parts // 2
    core, chip = me % 2, me // 2
    width = whole.shape[-1]
    packed = jnp.concatenate([p.reshape(chips, 2, -1, width) for p in pieces], axis=2)
    halves = whole.reshape(2, -1, width)

    def of_core(c):
        rows = lax.dynamic_index_in_dim(packed, c, 1, keepdims=False).reshape(-1, width)
        return jnp.concatenate([rows, lax.dynamic_index_in_dim(halves, c, 0, keepdims=False)])

    mine = of_core(core) + permute(of_core(1 - core), 1, parts)
    (mine,) = wait_for([mine], after)
    size = packed.shape[2]
    rows = mine[: chips * size].reshape(chips, size, width)
    half = mine[chips * size :]

    def of_chip(c):
        return jnp.concatenate([lax.dynamic_index_in_dim(rows, c, 0, keepdims=False), half])

    total = of_chip(chip)
    for e in range(1, chips):
        total = total + permute(of_chip(chip ^ e), 2 * e, parts)
    (later,) = wait_for([total], [last])
    summed, half = later[:size], later[size:]
    d = 1
    while d < tensors:
        summed = summed + permute(summed, d, tensors, "tensor")
        d *= 2
    other = permute(half, 1, parts)
    whole = jnp.where(core == 0, jnp.concatenate([half, other]), jnp.concatenate([other, half]))
    out, start = [], 0
    for p in pieces:
        rows = p.size // parts // width
        out.append(summed[start : start + rows].reshape(-1, p.shape[1]))
        start += rows
    return out, whole, total


def sum_halves(term, me, parts):
    core = me % 2
    half = term.shape[0] // 2
    term = term + permute(term, 1, parts)
    return lax.dynamic_slice_in_dim(term, core * half, half, 0)


def sum_all(mine, me, parts, after):
    (mine,) = wait_for([mine], after)
    total = mine
    for e in range(1, parts // 2):
        total = total + permute(mine, 2 * e, parts)
    other = permute(total, 1, parts)
    return jnp.where(
        me % 2 == 0, jnp.concatenate([total, other]), jnp.concatenate([other, total])
    )


def body(parts, tensors, inputs, kernel, w_in, w_gate, w_out, factor_a, factor_b, cotangent):
    rows, chans = inputs.shape
    inner = factor_a.shape[0]
    blocks = rows // inner
    span = inner // parts
    me = lax.axis_index("tm").astype(jnp.int32)
    me1 = me[None]
    x3 = inputs.reshape(blocks, inner, chans)
    kn3 = kernel.reshape(blocks, inner, chans)
    ct3 = cotangent.reshape(blocks, inner, chans)
    factor_at = factor_a.T
    dist = distances(parts)
    partners = [(me ^ d)[None] for d in dist]

    spread = jnp.concatenate([p * blocks + jnp.arange(blocks, dtype=jnp.int32) for p in partners])
    fb = jnp.take(jnp.take(factor_b, spread, axis=0), spread, axis=1)

    received, window = [], 5
    gs_out = [grad_second_call(p, x3, ct3, w_gate, w_out, span, ()) for p in partners]
    gs_in = send(dist, gs_out, received, window, parts)
    tw_out = twisted_call(me1, x3, kn3, w_in, factor_at, dist, ())
    tw_in = send(dist, tw_out, received, window, parts)
    gt_out = grad_twisted_call(fb, gs_in)
    gt_in = send(dist, gt_out, received, window, parts)
    se_out, fb_term = second_call(fb.T, tw_in, gs_in)
    gk, gm, fa_term, gwi_term = grad_mixed_call(
        me1, x3, kn3, w_in, factor_at, factor_a, dist, gt_in
    )
    se_out = list(se_out)
    tail = 2 * (parts - 1) // 7
    se_out[-tail - 1 :] = wait_for(se_out[-tail - 1 :], [gwi_term])
    se_in = send(dist[:-tail], se_out[:-tail], received, window, parts)
    last = wait_for(se_out[-tail:], se_in[1 : parts // 2])
    se_in += [permute(a, d, parts) for a, d in zip(last, dist[-tail:])]
    state = ()
    for i, (partner, second) in enumerate(zip(partners, se_in)):
        if i == parts - 2:
            (second,) = wait_for([second], se_in[-1:] + list(state[2:]))
        if i == 1:
            early = state[2:]
        if i == parts - 1:
            middle = state[2:]
        state = outputs_call(partner, x3, ct3, gm, second, w_in, w_gate, w_out, state)
    outputs, grad_inputs, gw_term = state

    place = jnp.asarray([dist.index(d) for d in range(parts)], jnp.int32)
    natural = place[me ^ jnp.arange(parts, dtype=jnp.int32)]
    back = (natural[:, None] * blocks + jnp.arange(blocks, dtype=jnp.int32)).reshape(-1)
    fb_term = jnp.take(jnp.take(fb_term, back, axis=0), back, axis=1)
    fa_term, fb_term, gwi_term = wait_for([fa_term, fb_term, gwi_term], early)
    gw_half = sum_halves(gw_term, me, parts)
    (fa_sum, fb_sum), summed_in, total = sum_terms(
        [fa_term, fb_term], gwi_term.reshape(-1, w_in.shape[1]), me, parts, tensors, middle, gw_half
    )
    token_scale = 1.0 / math.sqrt(N1 * N2)
    grad_factor_a = fa_sum / math.sqrt(N1 * D)
    grad_factor_b = fb_sum / math.sqrt(N2 * D)
    summed_in = summed_in.reshape(w_in.shape)
    summed = sum_all(gw_half, me, parts, [total])
    summed_gate, summed_out = jnp.split(summed, 2)
    return (
        outputs.reshape(rows, chans),
        grad_inputs.reshape(rows, chans),
        gk.reshape(rows, chans),
        summed_in * token_scale,
        summed_gate * token_scale,
        summed_out * token_scale,
        grad_factor_a,
        grad_factor_b,
    )


def solution(mesh):
    return jax.shard_map(
        functools.partial(body, mesh.shape["tm"], mesh.shape["tensor"]),
        mesh=mesh,
        in_specs=(
            P("tm", "tensor"),
            P("tm", "tensor"),
            P("tensor", None, None),
            P("tensor", None, None),
            P("tensor", None, None),
            P(),
            P(),
            P("tm", "tensor"),
        ),
        out_specs=(
            P("tm", "tensor"),
            P("tm", "tensor"),
            P("tm", "tensor"),
            P("tensor", None, None),
            P("tensor", None, None),
            P("tensor", None, None),
            P("tm", None),
            P("tm", None),
        ),
        check_vma=False,
    )
```

```python
import functools
import math

import jax
import jax.numpy as jnp
from jax import lax
from jax.experimental import pallas as pl
from jax.experimental.pallas import tpu as pltpu
from jax.sharding import PartitionSpec as P

D = 1536
N1 = 256
N2 = 512
BF = jnp.bfloat16
F32 = jnp.float32
VMEM_LIMIT = 56 * 1024 * 1024
COST = 0.1


def dot(left, right):
    return jnp.dot(left, right, preferred_element_type=F32)


def dot_nt(left, right):
    return lax.dot_general(left, right, (((1,), (1,)), ((), ())), preferred_element_type=F32)


def dot_tn(left, right):
    return lax.dot_general(left, right, (((0,), (0,)), ((), ())), preferred_element_type=F32)


def diagonal(first, second):
    zero = jnp.zeros_like(first)
    return jnp.concatenate(
        [jnp.concatenate([first, zero], axis=1), jnp.concatenate([zero, second], axis=1)], axis=0
    )


def params(dims):
    return pltpu.CompilerParams(
        dimension_semantics=("arbitrary",) * dims, vmem_limit_bytes=VMEM_LIMIT
    )


def cost(flops, nbytes):
    return pl.CostEstimate(flops=int(flops * COST), bytes_accessed=int(nbytes * COST), transcendentals=0)


def stack_rows(pieces):
    if pieces[0].shape[0] % 16 == 0:
        return jnp.concatenate(pieces, axis=0)
    return jnp.concatenate([p.astype(F32) for p in pieces], axis=0).astype(BF)


def grad_second_kernel(p_ref, x_ref, ct_ref, wg_ref, wo_ref, *rest):
    out_ref = rest[-1]
    blocks, span, chans = x_ref.shape
    width = wg_ref.shape[1]
    rows = blocks * span
    for n in range(chans // width):
        lanes = slice(n * width, (n + 1) * width)
        x = x_ref[:, :, lanes].reshape(rows, width)
        ct = ct_ref[:, :, lanes].reshape(rows, width)
        both = dot(jnp.concatenate([x, ct], axis=1), diagonal(wg_ref[n], wo_ref[n].T))
        value = (both[:, :width] * both[:, width:]).astype(BF)
        out_ref[:, :, lanes] = jnp.swapaxes(value.reshape(blocks, span, width), 0, 1)


def grad_second_call(partner, x3, ct3, w_gate, w_out, span, after):
    blocks, inner, chans = x3.shape
    width = w_gate.shape[1]
    some = min(blocks, 16)
    rows = pl.BlockSpec((some, span, chans), lambda i, p: (i, p[0], 0))
    weight = pl.BlockSpec(w_gate.shape, lambda i, p: (0, 0, 0))
    anywhere = pl.BlockSpec(memory_space=pl.ANY)
    size = blocks * span * chans
    return pl.pallas_call(
        grad_second_kernel,
        grid_spec=pltpu.PrefetchScalarGridSpec(
            num_scalar_prefetch=1,
            grid=(blocks // some,),
            in_specs=[rows, rows, weight, weight] + [anywhere] * len(after),
            out_specs=pl.BlockSpec((span, some, chans), lambda i, p: (0, i, 0)),
        ),
        out_shape=jax.ShapeDtypeStruct((span, blocks, chans), BF),
        compiler_params=params(1),
        cost_estimate=cost(4 * size * width, 6 * size),
        name="grad_second",
    )(partner, x3, ct3, w_gate, w_out, *after)


def twisted_kernel(dist, me_ref, x_ref, kn_ref, wi_ref, at_ref, *rest):
    some, inner, width = x_ref.shape
    scr = rest[-1]
    blocks = scr.shape[0] // inner
    outs = rest[-1 - len(dist) : -1]
    span = inner // len(dist)
    step = pl.program_id(1)
    mixed = dot(x_ref[...].reshape(some * inner, width), wi_ref[0]).astype(BF)
    for q in range(0, some, 2):
        pair = jnp.concatenate(
            [mixed[q * inner : (q + 1) * inner], mixed[(q + 1) * inner : (q + 2) * inner]], axis=1
        )
        first = dot(at_ref[...], pair)
        for h in range(2):
            value = first[:, h * width : (h + 1) * width] * kn_ref[q + h].astype(F32)
            scr[pl.ds(step * some + q + h, inner, stride=blocks), :] = value

    @pl.when(step == pl.num_programs(1) - 1)
    def _():
        for d, out in zip(dist, outs):
            first_row = pl.multiple_of((me_ref[0] ^ d) * (span * blocks), span * blocks)
            piece = scr[pl.ds(first_row, span * blocks), :]
            out[...] = piece.reshape(span, blocks, width).astype(BF)


def twisted_call(me, x3, kn3, w_in, factor_at, dist, after):
    parts = len(dist)
    blocks, inner, chans = x3.shape
    width = w_in.shape[1]
    span = inner // parts
    some = 4
    rows = pl.BlockSpec((some, inner, width), lambda n, i, m: (i, 0, n))
    out = pl.BlockSpec((span, blocks, width), lambda n, i, m: (0, 0, n))
    size = blocks * inner * chans
    return pl.pallas_call(
        functools.partial(twisted_kernel, dist),
        grid_spec=pltpu.PrefetchScalarGridSpec(
            num_scalar_prefetch=1,
            grid=(chans // width, blocks // some),
            in_specs=[
                rows,
                rows,
                pl.BlockSpec((1, width, width), lambda n, i, m: (n, 0, 0)),
                pl.BlockSpec((inner, inner), lambda n, i, m: (0, 0)),
            ]
            + [pl.BlockSpec(memory_space=pl.ANY)] * len(after),
            out_specs=[out] * parts,
            scratch_shapes=[pltpu.VMEM((inner * blocks, width), F32)],
        ),
        out_shape=[jax.ShapeDtypeStruct((span, blocks, chans), BF)] * parts,
        compiler_params=params(2),
        cost_estimate=cost(2 * size * (width + inner), 6 * size),
        name="twisted",
    )(me, x3, kn3, w_in, factor_at, *after)


def grad_twisted_kernel(fb_ref, *refs):
    parts = len(refs) // 2
    ins, outs = refs[:parts], refs[parts:]
    some, blocks, _ = ins[0].shape
    for k in range(some):
        value = dot(fb_ref[...], stack_rows([ref[k] for ref in ins])).astype(BF)
        for d in range(parts):
            outs[d][k] = value[d * blocks : (d + 1) * blocks]


def grad_twisted_call(fb, arrays):
    parts = len(arrays)
    span, blocks, chans = arrays[0].shape
    some = 8
    spec = pl.BlockSpec((some, blocks, chans), lambda k: (k, 0, 0))
    size = parts * span * blocks * chans
    return pl.pallas_call(
        grad_twisted_kernel,
        grid=(span // some,),
        in_specs=[pl.BlockSpec(fb.shape, lambda k: (0, 0))] + [spec] * parts,
        out_specs=[spec] * parts,
        out_shape=[jax.ShapeDtypeStruct((span, blocks, chans), BF)] * parts,
        compiler_params=params(1),
        cost_estimate=cost(2 * size * fb.shape[0], 4 * size),
        name="grad_twisted",
    )(fb, *arrays)


def second_kernel(fbt_ref, *refs):
    parts = (len(refs) - 1) // 3
    tws, gss, outs, fbg = refs[:parts], refs[parts : 2 * parts], refs[2 * parts : -1], refs[-1]
    some, blocks, _ = tws[0].shape

    @pl.when(pl.program_id(0) == 0)
    def _():
        fbg[...] = jnp.zeros_like(fbg)

    for k in range(some):
        tw = stack_rows([ref[k] for ref in tws])
        gs = stack_rows([ref[k] for ref in gss])
        value = dot(fbt_ref[...], tw).astype(BF)
        for d in range(parts):
            outs[d][k] = value[d * blocks : (d + 1) * blocks]
        fbg[...] += dot_nt(tw, gs)


def second_call(fbt, tws, gss):
    parts = len(tws)
    span, blocks, chans = tws[0].shape
    some = 8
    spec = pl.BlockSpec((some, blocks, chans), lambda k: (k, 0, 0))
    whole = pl.BlockSpec(fbt.shape, lambda k: (0, 0))
    size = parts * span * blocks * chans
    result = pl.pallas_call(
        second_kernel,
        grid=(span // some,),
        in_specs=[whole] + [spec] * (2 * parts),
        out_specs=[spec] * parts + [whole],
        out_shape=[jax.ShapeDtypeStruct((span, blocks, chans), BF)] * parts
        + [jax.ShapeDtypeStruct(fbt.shape, F32)],
        compiler_params=params(1),
        cost_estimate=cost(4 * size * fbt.shape[0], 6 * size),
        name="second",
    )(fbt, *tws, *gss)
    return result[:-1], result[-1]


def grad_mixed_kernel(dist, me_ref, x_ref, kn_ref, wi_ref, at_ref, a_ref, *rest):
    gts = rest[:-5]
    gk_ref, gm_ref, fag, gwi, scr = rest[-5:]
    some, inner, width = x_ref.shape
    span, blocks, _ = gts[0].shape
    step = pl.program_id(1)

    @pl.when(step == 0)
    def _():
        gwi[...] = jnp.zeros_like(gwi)
        for d, ref in zip(dist, gts):
            first_row = pl.multiple_of((me_ref[0] ^ d) * (span * blocks), span * blocks)
            scr[pl.ds(first_row, span * blocks), :] = (
                ref[...].astype(F32).reshape(span * blocks, width)
            )

    @pl.when((step == 0) & (pl.program_id(0) == 0))
    def _():
        fag[...] = jnp.zeros_like(fag)

    x = x_ref[...].reshape(some * inner, width)
    mixed = dot(x, wi_ref[0]).astype(BF)
    for q in range(0, some, 2):
        pair = jnp.concatenate(
            [mixed[q * inner : (q + 1) * inner], mixed[(q + 1) * inner : (q + 2) * inner]], axis=1
        )
        first = dot(at_ref[...], pair)
        grads = []
        for h in range(2):
            gt = scr[pl.ds(step * some + q + h, inner, stride=blocks), :]
            gk_ref[q + h] = (gt * first[:, h * width : (h + 1) * width]).astype(BF)
            grads.append((gt * kn_ref[q + h].astype(F32)).astype(BF))
        grad_first = jnp.concatenate(grads, axis=1)
        fag[...] += dot_nt(pair, grad_first)
        grad_mixed = dot(a_ref[...], grad_first).astype(BF)
        for h in range(2):
            gm_ref[q + h] = grad_mixed[:, h * width : (h + 1) * width]
    gwi[0] += dot_tn(x, gm_ref[...].reshape(some * inner, width))


def grad_mixed_call(me, x3, kn3, w_in, factor_at, factor_a, dist, gts):
    parts = len(gts)
    blocks, inner, chans = x3.shape
    width = w_in.shape[1]
    span = inner // parts
    some = 4
    rows = pl.BlockSpec((some, inner, width), lambda n, i, m: (i, 0, n))
    weight = pl.BlockSpec((1, width, width), lambda n, i, m: (n, 0, 0))
    whole = pl.BlockSpec((inner, inner), lambda n, i, m: (0, 0))
    size = blocks * inner * chans
    return pl.pallas_call(
        functools.partial(grad_mixed_kernel, dist),
        grid_spec=pltpu.PrefetchScalarGridSpec(
            num_scalar_prefetch=1,
            grid=(chans // width, blocks // some),
            in_specs=[rows, rows, weight, whole, whole]
            + [pl.BlockSpec((span, blocks, width), lambda n, i, m: (0, 0, n))] * parts,
            out_specs=[rows, rows, whole, weight],
            scratch_shapes=[pltpu.VMEM((inner * blocks, width), F32)],
        ),
        out_shape=[
            jax.ShapeDtypeStruct(x3.shape, BF),
            jax.ShapeDtypeStruct(x3.shape, BF),
            jax.ShapeDtypeStruct((inner, inner), F32),
            jax.ShapeDtypeStruct(w_in.shape, F32),
        ],
        compiler_params=params(2),
        cost_estimate=cost(2 * size * (2 * width + 3 * inner), 10 * size),
        name="grad_mixed",
    )(me, x3, kn3, w_in, factor_at, factor_a, *gts)


def outputs_kernel(arrays, terms, p_ref, x_ref, ct_ref, se_ref, wg_ref, wo_ref, *rest):
    rest = list(rest)
    gm_ref, wi_ref = (rest.pop(0), rest.pop(0)) if arrays else (None, None)
    gw = rest.pop() if terms else None
    out_ref, gi_ref = rest[-2:] if arrays else (None, None)
    before = rest[:-2] if arrays else rest
    blocks, span, chans = x_ref.shape
    mixers, width, _ = wg_ref.shape
    rows = blocks * span

    if terms:

        @pl.when(pl.program_id(0) == 0)
        def _():
            gw[...] = before[-1][...] if before else jnp.zeros_like(gw)

    for n in range(mixers):
        lanes = slice(n * width, (n + 1) * width)
        x = x_ref[:, :, lanes].reshape(rows, width)
        ct = ct_ref[:, :, lanes].reshape(rows, width)
        second = jnp.swapaxes(se_ref[:, :, lanes], 0, 1).astype(F32).reshape(rows, width)
        both = dot(jnp.concatenate([x, ct], axis=1), diagonal(wg_ref[n], wo_ref[n].T))
        gated = (second * both[:, :width]).astype(BF)
        grad_gate = (both[:, width:] * second).astype(BF)
        if arrays:
            out_ref[:, :, lanes] = dot(gated, wo_ref[n]).astype(BF).reshape(blocks, span, width)
            grads = jnp.concatenate([gm_ref[:, :, lanes].reshape(rows, width), grad_gate], axis=1)
            back = jnp.concatenate([wi_ref[n].T, wg_ref[n].T], axis=0)
            gi_ref[:, :, lanes] = dot(grads, back).astype(BF).reshape(blocks, span, width)
        if terms:
            both = dot_tn(
                jnp.concatenate([x, gated], axis=1), jnp.concatenate([grad_gate, ct], axis=1)
            )
            gw[n] += both[:width, :width]
            gw[mixers + n] += both[width:, width:]


def outputs_call(partner, x3, ct3, gm3, second, w_in, w_gate, w_out, arrays=(), terms=()):
    blocks, inner, chans = x3.shape
    width = w_in.shape[1]
    span = second.shape[0]
    some = min(blocks, 16)
    rows = pl.BlockSpec((some, span, chans), lambda i, p: (i, p[0], 0))
    weight = pl.BlockSpec(w_in.shape, lambda i, p: (0, 0, 0))
    both = (2 * w_in.shape[0], width, width)
    grads = pl.BlockSpec(both, lambda i, p: (0, 0, 0))
    anywhere = pl.BlockSpec(memory_space=pl.ANY)
    size = blocks * span * chans
    operands = [x3, ct3, second, w_gate, w_out]
    specs = [rows, rows, pl.BlockSpec((span, some, chans), lambda i, p: (0, i, 0)), weight, weight]
    aliases, out_specs, out_shape = {}, [], []
    if arrays is not None:
        operands += [gm3, w_in]
        specs += [rows, weight]
        aliases = {len(operands) + 1 + i: i for i in range(len(arrays))}
        operands += arrays
        specs += [anywhere] * len(arrays)
        out_specs += [rows, rows]
        out_shape += [jax.ShapeDtypeStruct(x3.shape, BF)] * 2
    if terms is not None:
        operands += terms
        specs += [grads] * len(terms)
        out_specs += [grads]
        out_shape += [jax.ShapeDtypeStruct(both, F32)]
    return pl.pallas_call(
        functools.partial(outputs_kernel, arrays is not None, terms is not None),
        grid_spec=pltpu.PrefetchScalarGridSpec(
            num_scalar_prefetch=1, grid=(blocks // some,), in_specs=specs, out_specs=out_specs
        ),
        out_shape=out_shape,
        input_output_aliases=aliases,
        compiler_params=params(1),
        cost_estimate=cost(14 * size * width, 12 * size),
        name="outputs",
    )(partner, *operands)


def nothing_kernel(*refs):
    pass


def wait_for(arrays, after):
    anywhere = pl.BlockSpec(memory_space=pl.ANY)
    return pl.pallas_call(
        nothing_kernel,
        in_specs=[anywhere] * (len(arrays) + len(after)),
        out_specs=[anywhere] * len(arrays),
        out_shape=[jax.ShapeDtypeStruct(a.shape, a.dtype) for a in arrays],
        input_output_aliases={i: i for i in range(len(arrays))},
        compiler_params=pltpu.CompilerParams(vmem_limit_bytes=VMEM_LIMIT),
        name="wait_for",
    )(*arrays, *after)


def permute(array, d, parts, axis="tm"):
    return lax.ppermute(array, axis, [(i, i ^ d) for i in range(parts)])


def distances(parts):
    far = sorted(range(2, parts), key=lambda d: (-bin(d >> 1).count("1"), -(d & 1), -d))
    cut = 4 * (parts - 1) // 7
    return [0] + far[:cut] + [1] + far[cut:]


def send(dist, arrays, received, window, parts):
    into = [arrays[0]]
    for d, array in zip(dist[1:], arrays[1:]):
        if len(received) >= window:
            (array,) = wait_for([array], [received[-window]])
        received.append(permute(array, d, parts))
        into.append(received[-1])
    return into


def sum_terms(pieces, whole, me, parts, tensors, after, last):
    chips = parts // 2
    core, chip = me % 2, me // 2
    width = whole.shape[-1]
    packed = jnp.concatenate([p.reshape(chips, 2, -1, width) for p in pieces], axis=2)
    halves = whole.reshape(2, -1, width)

    def of_core(c):
        rows = lax.dynamic_index_in_dim(packed, c, 1, keepdims=False).reshape(-1, width)
        return jnp.concatenate([rows, lax.dynamic_index_in_dim(halves, c, 0, keepdims=False)])

    mine = of_core(core) + permute(of_core(1 - core), 1, parts)
    (mine,) = wait_for([mine], after)
    size = packed.shape[2]
    rows = mine[: chips * size].reshape(chips, size, width)
    half = mine[chips * size :]

    def of_chip(c):
        return jnp.concatenate([lax.dynamic_index_in_dim(rows, c, 0, keepdims=False), half])

    summed = lax.dynamic_index_in_dim(rows, chip, 0, keepdims=False)
    others = [permute(of_chip(chip ^ e), 2 * e, parts) for e in range(1, chips)]
    for other in wait_for(others, []):
        summed, half = summed + other[:size], half + other[size:]
    total = [summed, half]
    summed, half = wait_for(total, [last])
    d = 1
    while 2 * d < tensors:
        summed = summed + permute(summed, d, tensors, "tensor")
        d *= 2
    beside = permute(summed, d, tensors, "tensor") if d < tensors else jnp.zeros_like(summed)
    other = permute(half, 1, parts)
    return total, [summed, beside], [half, other]


def unpack(pieces, rows, halves, me, parts, after):
    summed, beside, half, other = wait_for(list(rows) + list(halves), after)
    summed = summed + beside
    out, start = [], 0
    for p in pieces:
        size = p.size // parts // summed.shape[1]
        out.append(summed[start : start + size].reshape(-1, p.shape[1]))
        start += size
    first, second = jnp.where(me % 2 == 0, half, other), jnp.where(me % 2 == 0, other, half)
    return out, jnp.concatenate([first, second])


def sum_halves(term, me, parts, scale):
    core = me % 2
    half = term.shape[0] // 2
    term = term + permute(term, 1, parts)
    return lax.dynamic_slice_in_dim(term, core * half, half, 0) * scale


def send_halves(mine, parts, after):
    (mine,) = wait_for([mine], after)
    return [mine] + [permute(mine, 2 * e, parts) for e in range(1, parts // 2)]


def sum_all(halves, me, parts, after):
    halves = wait_for(halves, after)
    total = halves[0]
    for half in halves[1:]:
        total = total + half
    other = permute(total, 1, parts)
    return jnp.where(
        me % 2 == 0, jnp.concatenate([total, other]), jnp.concatenate([other, total])
    )


def body(parts, tensors, inputs, kernel, w_in, w_gate, w_out, factor_a, factor_b, cotangent):
    rows, chans = inputs.shape
    inner = factor_a.shape[0]
    blocks = rows // inner
    span = inner // parts
    me = lax.axis_index("tm").astype(jnp.int32)
    me1 = me[None]
    x3 = inputs.reshape(blocks, inner, chans)
    kn3 = kernel.reshape(blocks, inner, chans)
    ct3 = cotangent.reshape(blocks, inner, chans)
    factor_at = factor_a.T
    dist = distances(parts)
    partners = [(me ^ d)[None] for d in dist]

    spread = jnp.concatenate([p * blocks + jnp.arange(blocks, dtype=jnp.int32) for p in partners])
    fb = jnp.take(jnp.take(factor_b, spread, axis=0), spread, axis=1)

    received, window = [], 5
    gs_out = [grad_second_call(p, x3, ct3, w_gate, w_out, span, ()) for p in partners]
    gs_in = send(dist, gs_out, received, window, parts)
    tw_out = twisted_call(me1, x3, kn3, w_in, factor_at, dist, ())
    tw_in = send(dist, tw_out, received, window, parts)
    gt_out = grad_twisted_call(fb, gs_in)
    gt_in = send(dist, gt_out, received, window, parts)
    se_out, fb_term = second_call(fb.T, tw_in, gs_in)
    gk, gm, fa_term, gwi_term = grad_mixed_call(
        me1, x3, kn3, w_in, factor_at, factor_a, dist, gt_in
    )
    se_out = list(se_out)
    tail = 2 * (parts - 1) // 7
    se_out[-tail - 1 :] = wait_for(se_out[-tail - 1 :], [gwi_term])
    se_in = send(dist[:-tail], se_out[:-tail], received, window, parts)
    last = wait_for(se_out[-tail:], se_in[1 : 1 + parts // 4])
    se_in += [permute(a, d, parts) for a, d in zip(last, dist[-tail:])]
    arrays, terms = (), ()
    late = parts - tail
    for i in range(late):
        *arrays, term = outputs_call(
            partners[i], x3, ct3, gm, se_in[i], w_in, w_gate, w_out, arrays, terms
        )
        terms = [term]
        if i == 1:
            early = terms
    middle = se_in[late:] + terms
    for i in range(late, parts):
        terms = outputs_call(
            partners[i], x3, ct3, gm, se_in[i], w_in, w_gate, w_out, None, terms
        )
    (gw_term,) = terms
    place = jnp.asarray([dist.index(d) for d in range(parts)], jnp.int32)
    natural = place[me ^ jnp.arange(parts, dtype=jnp.int32)]
    back = (natural[:, None] * blocks + jnp.arange(blocks, dtype=jnp.int32)).reshape(-1)
    fb_term = jnp.take(jnp.take(fb_term, back, axis=0), back, axis=1)
    fa_term, fb_term, gwi_term = wait_for([fa_term, fb_term, gwi_term], early)
    token_scale = 1.0 / math.sqrt(N1 * N2)
    gw_half = sum_halves(gw_term, me, parts, token_scale)
    pieces = [fa_term / math.sqrt(N1 * D), fb_term / math.sqrt(N2 * D)]
    total, in_rows, in_halves = sum_terms(
        pieces,
        gwi_term.reshape(-1, w_in.shape[1]) * token_scale,
        me,
        parts,
        tensors,
        middle,
        gw_half,
    )
    halves = send_halves(gw_half, parts, [])
    se_in[late:] = wait_for(se_in[late:], in_rows[:1])
    for i in range(late, parts):
        arrays = outputs_call(
            partners[i], x3, ct3, gm, se_in[i], w_in, w_gate, w_out, arrays, None
        )
    outputs, grad_inputs = arrays
    summed = sum_all(halves, me, parts, arrays)
    (fa_sum, fb_sum), summed_in = unpack(pieces, in_rows, in_halves, me, parts, arrays)
    summed_in = summed_in.reshape(w_in.shape)
    summed_gate, summed_out = jnp.split(summed, 2)
    return (
        outputs.reshape(rows, chans),
        grad_inputs.reshape(rows, chans),
        gk.reshape(rows, chans),
        summed_in,
        summed_gate,
        summed_out,
        fa_sum,
        fb_sum,
    )


def solution(mesh):
    return jax.shard_map(
        functools.partial(body, mesh.shape["tm"], mesh.shape["tensor"]),
        mesh=mesh,
        in_specs=(
            P("tm", "tensor"),
            P("tm", "tensor"),
            P("tensor", None, None),
            P("tensor", None, None),
            P("tensor", None, None),
            P(),
            P(),
            P("tm", "tensor"),
        ),
        out_specs=(
            P("tm", "tensor"),
            P("tm", "tensor"),
            P("tm", "tensor"),
            P("tensor", None, None),
            P("tensor", None, None),
            P("tensor", None, None),
            P("tm", None),
            P("tm", None),
        ),
        check_vma=False,
    )
```

```python
import functools
import math

import jax
import jax.numpy as jnp
from jax import lax
from jax.experimental import pallas as pl
from jax.experimental.pallas import tpu as pltpu
from jax.sharding import PartitionSpec as P

D = 1536
N1 = 256
N2 = 512
BF = jnp.bfloat16
F32 = jnp.float32
VMEM_LIMIT = 56 * 1024 * 1024
COST = 0.1


def dot(left, right):
    return jnp.dot(left, right, preferred_element_type=F32)


def dot_nt(left, right):
    return lax.dot_general(left, right, (((1,), (1,)), ((), ())), preferred_element_type=F32)


def dot_tn(left, right):
    return lax.dot_general(left, right, (((0,), (0,)), ((), ())), preferred_element_type=F32)


def diagonal(first, second):
    zero = jnp.zeros_like(first)
    return jnp.concatenate(
        [jnp.concatenate([first, zero], axis=1), jnp.concatenate([zero, second], axis=1)], axis=0
    )


def params(dims):
    return pltpu.CompilerParams(
        dimension_semantics=("arbitrary",) * dims, vmem_limit_bytes=VMEM_LIMIT
    )


def cost(flops, nbytes):
    return pl.CostEstimate(flops=int(flops * COST), bytes_accessed=int(nbytes * COST), transcendentals=0)


def stack_rows(pieces):
    if pieces[0].shape[0] % 16 == 0:
        return jnp.concatenate(pieces, axis=0)
    return jnp.concatenate([p.astype(F32) for p in pieces], axis=0).astype(BF)


def grad_second_kernel(p_ref, x_ref, ct_ref, wg_ref, wo_ref, *rest):
    out_ref = rest[-1]
    blocks, span, chans = x_ref.shape
    width = wg_ref.shape[1]
    rows = blocks * span
    for n in range(chans // width):
        lanes = slice(n * width, (n + 1) * width)
        x = x_ref[:, :, lanes].reshape(rows, width)
        ct = ct_ref[:, :, lanes].reshape(rows, width)
        both = dot(jnp.concatenate([x, ct], axis=1), diagonal(wg_ref[n], wo_ref[n].T))
        value = (both[:, :width] * both[:, width:]).astype(BF)
        out_ref[:, :, lanes] = jnp.swapaxes(value.reshape(blocks, span, width), 0, 1)


def grad_second_call(partner, x3, ct3, w_gate, w_out, span, after):
    blocks, inner, chans = x3.shape
    width = w_gate.shape[1]
    some = min(blocks, 16)
    rows = pl.BlockSpec((some, span, chans), lambda i, p: (i, p[0], 0))
    weight = pl.BlockSpec(w_gate.shape, lambda i, p: (0, 0, 0))
    anywhere = pl.BlockSpec(memory_space=pl.ANY)
    size = blocks * span * chans
    return pl.pallas_call(
        grad_second_kernel,
        grid_spec=pltpu.PrefetchScalarGridSpec(
            num_scalar_prefetch=1,
            grid=(blocks // some,),
            in_specs=[rows, rows, weight, weight] + [anywhere] * len(after),
            out_specs=pl.BlockSpec((span, some, chans), lambda i, p: (0, i, 0)),
        ),
        out_shape=jax.ShapeDtypeStruct((span, blocks, chans), BF),
        compiler_params=params(1),
        cost_estimate=cost(4 * size * width, 6 * size),
        name="grad_second",
    )(partner, x3, ct3, w_gate, w_out, *after)


def twisted_kernel(dist, me_ref, x_ref, kn_ref, wi_ref, at_ref, *rest):
    some, inner, width = x_ref.shape
    scr = rest[-1]
    blocks = scr.shape[0] // inner
    outs = rest[-1 - len(dist) : -1]
    span = inner // len(dist)
    step = pl.program_id(1)
    mixed = dot(x_ref[...].reshape(some * inner, width), wi_ref[0]).astype(BF)
    for q in range(0, some, 2):
        pair = jnp.concatenate(
            [mixed[q * inner : (q + 1) * inner], mixed[(q + 1) * inner : (q + 2) * inner]], axis=1
        )
        first = dot(at_ref[...], pair)
        for h in range(2):
            value = first[:, h * width : (h + 1) * width] * kn_ref[q + h].astype(F32)
            scr[pl.ds(step * some + q + h, inner, stride=blocks), :] = value

    @pl.when(step == pl.num_programs(1) - 1)
    def _():
        for d, out in zip(dist, outs):
            first_row = pl.multiple_of((me_ref[0] ^ d) * (span * blocks), span * blocks)
            piece = scr[pl.ds(first_row, span * blocks), :]
            out[...] = piece.reshape(span, blocks, width).astype(BF)


def twisted_call(me, x3, kn3, w_in, factor_at, dist, after):
    parts = len(dist)
    blocks, inner, chans = x3.shape
    width = w_in.shape[1]
    span = inner // parts
    some = 4
    rows = pl.BlockSpec((some, inner, width), lambda n, i, m: (i, 0, n))
    out = pl.BlockSpec((span, blocks, width), lambda n, i, m: (0, 0, n))
    size = blocks * inner * chans
    return pl.pallas_call(
        functools.partial(twisted_kernel, dist),
        grid_spec=pltpu.PrefetchScalarGridSpec(
            num_scalar_prefetch=1,
            grid=(chans // width, blocks // some),
            in_specs=[
                rows,
                rows,
                pl.BlockSpec((1, width, width), lambda n, i, m: (n, 0, 0)),
                pl.BlockSpec((inner, inner), lambda n, i, m: (0, 0)),
            ]
            + [pl.BlockSpec(memory_space=pl.ANY)] * len(after),
            out_specs=[out] * parts,
            scratch_shapes=[pltpu.VMEM((inner * blocks, width), F32)],
        ),
        out_shape=[jax.ShapeDtypeStruct((span, blocks, chans), BF)] * parts,
        compiler_params=params(2),
        cost_estimate=cost(2 * size * (width + inner), 6 * size),
        name="twisted",
    )(me, x3, kn3, w_in, factor_at, *after)


def grad_twisted_kernel(fb_ref, *refs):
    parts = len(refs) // 2
    ins, outs = refs[:parts], refs[parts:]
    some, blocks, _ = ins[0].shape
    for k in range(some):
        value = dot(fb_ref[...], stack_rows([ref[k] for ref in ins])).astype(BF)
        for d in range(parts):
            outs[d][k] = value[d * blocks : (d + 1) * blocks]


def grad_twisted_call(fb, arrays):
    parts = len(arrays)
    span, blocks, chans = arrays[0].shape
    some = 8
    spec = pl.BlockSpec((some, blocks, chans), lambda k: (k, 0, 0))
    size = parts * span * blocks * chans
    return pl.pallas_call(
        grad_twisted_kernel,
        grid=(span // some,),
        in_specs=[pl.BlockSpec(fb.shape, lambda k: (0, 0))] + [spec] * parts,
        out_specs=[spec] * parts,
        out_shape=[jax.ShapeDtypeStruct((span, blocks, chans), BF)] * parts,
        compiler_params=params(1),
        cost_estimate=cost(2 * size * fb.shape[0], 4 * size),
        name="grad_twisted",
    )(fb, *arrays)


def second_kernel(fbt_ref, *refs):
    parts = (len(refs) - 1) // 3
    tws, gss, outs, fbg = refs[:parts], refs[parts : 2 * parts], refs[2 * parts : -1], refs[-1]
    some, blocks, _ = tws[0].shape

    @pl.when(pl.program_id(0) == 0)
    def _():
        fbg[...] = jnp.zeros_like(fbg)

    for k in range(some):
        tw = stack_rows([ref[k] for ref in tws])
        gs = stack_rows([ref[k] for ref in gss])
        value = dot(fbt_ref[...], tw).astype(BF)
        for d in range(parts):
            outs[d][k] = value[d * blocks : (d + 1) * blocks]
        fbg[...] += dot_nt(tw, gs)


def second_call(fbt, tws, gss):
    parts = len(tws)
    span, blocks, chans = tws[0].shape
    some = 8
    spec = pl.BlockSpec((some, blocks, chans), lambda k: (k, 0, 0))
    whole = pl.BlockSpec(fbt.shape, lambda k: (0, 0))
    size = parts * span * blocks * chans
    result = pl.pallas_call(
        second_kernel,
        grid=(span // some,),
        in_specs=[whole] + [spec] * (2 * parts),
        out_specs=[spec] * parts + [whole],
        out_shape=[jax.ShapeDtypeStruct((span, blocks, chans), BF)] * parts
        + [jax.ShapeDtypeStruct(fbt.shape, F32)],
        compiler_params=params(1),
        cost_estimate=cost(4 * size * fbt.shape[0], 6 * size),
        name="second",
    )(fbt, *tws, *gss)
    return result[:-1], result[-1]


def grad_mixed_kernel(dist, me_ref, x_ref, kn_ref, wi_ref, at_ref, a_ref, *rest):
    gts = rest[:-5]
    gk_ref, gm_ref, fag, gwi, scr = rest[-5:]
    some, inner, width = x_ref.shape
    span, blocks, _ = gts[0].shape
    step = pl.program_id(1)

    @pl.when(step == 0)
    def _():
        gwi[...] = jnp.zeros_like(gwi)
        for d, ref in zip(dist, gts):
            first_row = pl.multiple_of((me_ref[0] ^ d) * (span * blocks), span * blocks)
            scr[pl.ds(first_row, span * blocks), :] = (
                ref[...].astype(F32).reshape(span * blocks, width)
            )

    @pl.when((step == 0) & (pl.program_id(0) == 0))
    def _():
        fag[...] = jnp.zeros_like(fag)

    x = x_ref[...].reshape(some * inner, width)
    mixed = dot(x, wi_ref[0]).astype(BF)
    for q in range(0, some, 2):
        pair = jnp.concatenate(
            [mixed[q * inner : (q + 1) * inner], mixed[(q + 1) * inner : (q + 2) * inner]], axis=1
        )
        first = dot(at_ref[...], pair)
        grads = []
        for h in range(2):
            gt = scr[pl.ds(step * some + q + h, inner, stride=blocks), :]
            gk_ref[q + h] = (gt * first[:, h * width : (h + 1) * width]).astype(BF)
            grads.append((gt * kn_ref[q + h].astype(F32)).astype(BF))
        grad_first = jnp.concatenate(grads, axis=1)
        fag[...] += dot_nt(pair, grad_first)
        grad_mixed = dot(a_ref[...], grad_first).astype(BF)
        for h in range(2):
            gm_ref[q + h] = grad_mixed[:, h * width : (h + 1) * width]
    gwi[0] += dot_tn(x, gm_ref[...].reshape(some * inner, width))


def grad_mixed_call(me, x3, kn3, w_in, factor_at, factor_a, dist, gts):
    parts = len(gts)
    blocks, inner, chans = x3.shape
    width = w_in.shape[1]
    span = inner // parts
    some = 4
    rows = pl.BlockSpec((some, inner, width), lambda n, i, m: (i, 0, n))
    weight = pl.BlockSpec((1, width, width), lambda n, i, m: (n, 0, 0))
    whole = pl.BlockSpec((inner, inner), lambda n, i, m: (0, 0))
    size = blocks * inner * chans
    return pl.pallas_call(
        functools.partial(grad_mixed_kernel, dist),
        grid_spec=pltpu.PrefetchScalarGridSpec(
            num_scalar_prefetch=1,
            grid=(chans // width, blocks // some),
            in_specs=[rows, rows, weight, whole, whole]
            + [pl.BlockSpec((span, blocks, width), lambda n, i, m: (0, 0, n))] * parts,
            out_specs=[rows, rows, whole, weight],
            scratch_shapes=[pltpu.VMEM((inner * blocks, width), F32)],
        ),
        out_shape=[
            jax.ShapeDtypeStruct(x3.shape, BF),
            jax.ShapeDtypeStruct(x3.shape, BF),
            jax.ShapeDtypeStruct((inner, inner), F32),
            jax.ShapeDtypeStruct(w_in.shape, F32),
        ],
        compiler_params=params(2),
        cost_estimate=cost(2 * size * (2 * width + 3 * inner), 10 * size),
        name="grad_mixed",
    )(me, x3, kn3, w_in, factor_at, factor_a, *gts)


def outputs_kernel(arrays, terms, p_ref, x_ref, ct_ref, se_ref, wg_ref, wo_ref, *rest):
    rest = list(rest)
    gm_ref, wi_ref = (rest.pop(0), rest.pop(0)) if arrays else (None, None)
    gw = rest.pop() if terms else None
    out_ref, gi_ref = rest[-2:] if arrays else (None, None)
    before = rest[:-2] if arrays else rest
    blocks, span, chans = x_ref.shape
    mixers, width, _ = wg_ref.shape
    rows = blocks * span

    if terms:

        @pl.when(pl.program_id(0) == 0)
        def _():
            gw[...] = before[-1][...] if before else jnp.zeros_like(gw)

    for n in range(mixers):
        lanes = slice(n * width, (n + 1) * width)
        x = x_ref[:, :, lanes].reshape(rows, width)
        ct = ct_ref[:, :, lanes].reshape(rows, width)
        second = jnp.swapaxes(se_ref[:, :, lanes], 0, 1).astype(F32).reshape(rows, width)
        both = dot(jnp.concatenate([x, ct], axis=1), diagonal(wg_ref[n], wo_ref[n].T))
        gated = (second * both[:, :width]).astype(BF)
        grad_gate = (both[:, width:] * second).astype(BF)
        if arrays:
            out_ref[:, :, lanes] = dot(gated, wo_ref[n]).astype(BF).reshape(blocks, span, width)
            grads = jnp.concatenate([gm_ref[:, :, lanes].reshape(rows, width), grad_gate], axis=1)
            back = jnp.concatenate([wi_ref[n].T, wg_ref[n].T], axis=0)
            gi_ref[:, :, lanes] = dot(grads, back).astype(BF).reshape(blocks, span, width)
        if terms:
            both = dot_tn(
                jnp.concatenate([x, gated], axis=1), jnp.concatenate([grad_gate, ct], axis=1)
            )
            gw[n] += both[:width, :width]
            gw[mixers + n] += both[width:, width:]


def outputs_call(partner, x3, ct3, gm3, second, w_in, w_gate, w_out, arrays=(), terms=()):
    blocks, inner, chans = x3.shape
    width = w_in.shape[1]
    span = second.shape[0]
    some = min(blocks, 16)
    rows = pl.BlockSpec((some, span, chans), lambda i, p: (i, p[0], 0))
    weight = pl.BlockSpec(w_in.shape, lambda i, p: (0, 0, 0))
    both = (2 * w_in.shape[0], width, width)
    grads = pl.BlockSpec(both, lambda i, p: (0, 0, 0))
    anywhere = pl.BlockSpec(memory_space=pl.ANY)
    size = blocks * span * chans
    operands = [x3, ct3, second, w_gate, w_out]
    specs = [rows, rows, pl.BlockSpec((span, some, chans), lambda i, p: (0, i, 0)), weight, weight]
    aliases, out_specs, out_shape = {}, [], []
    if arrays is not None:
        operands += [gm3, w_in]
        specs += [rows, weight]
        aliases = {len(operands) + 1 + i: i for i in range(len(arrays))}
        operands += arrays
        specs += [anywhere] * len(arrays)
        out_specs += [rows, rows]
        out_shape += [jax.ShapeDtypeStruct(x3.shape, BF)] * 2
    if terms is not None:
        operands += terms
        specs += [grads] * len(terms)
        out_specs += [grads]
        out_shape += [jax.ShapeDtypeStruct(both, F32)]
    return pl.pallas_call(
        functools.partial(outputs_kernel, arrays is not None, terms is not None),
        grid_spec=pltpu.PrefetchScalarGridSpec(
            num_scalar_prefetch=1, grid=(blocks // some,), in_specs=specs, out_specs=out_specs
        ),
        out_shape=out_shape,
        input_output_aliases=aliases,
        compiler_params=params(1),
        cost_estimate=cost(14 * size * width, 12 * size),
        name="outputs",
    )(partner, *operands)


def nothing_kernel(*refs):
    pass


def wait_for(arrays, after):
    anywhere = pl.BlockSpec(memory_space=pl.ANY)
    return pl.pallas_call(
        nothing_kernel,
        in_specs=[anywhere] * (len(arrays) + len(after)),
        out_specs=[anywhere] * len(arrays),
        out_shape=[jax.ShapeDtypeStruct(a.shape, a.dtype) for a in arrays],
        input_output_aliases={i: i for i in range(len(arrays))},
        compiler_params=pltpu.CompilerParams(vmem_limit_bytes=VMEM_LIMIT),
        name="wait_for",
    )(*arrays, *after)


def permute(array, d, parts, axis="tm"):
    return lax.ppermute(array, axis, [(i, i ^ d) for i in range(parts)])


def distances(parts):
    far = sorted(range(2, parts), key=lambda d: (-bin(d >> 1).count("1"), -(d & 1), -d))
    cut = 4 * (parts - 1) // 7
    return [0] + far[:cut] + [1] + far[cut:]


def send(dist, arrays, received, window, parts):
    into = [arrays[0]]
    for d, array in zip(dist[1:], arrays[1:]):
        if len(received) >= window:
            (array,) = wait_for([array], [received[-window]])
        received.append(permute(array, d, parts))
        into.append(received[-1])
    return into


def sum_cores(pieces, whole, me, parts):
    chips = parts // 2
    core = me % 2
    width = whole.shape[-1]
    packed = jnp.concatenate([p.reshape(chips, 2, -1, width) for p in pieces], axis=2)
    halves = whole.reshape(2, -1, width)

    def of_core(c):
        rows = lax.dynamic_index_in_dim(packed, c, 1, keepdims=False).reshape(-1, width)
        return jnp.concatenate([rows, lax.dynamic_index_in_dim(halves, c, 0, keepdims=False)])

    mine = of_core(core) + permute(of_core(1 - core), 1, parts)
    size = chips * packed.shape[2]
    return mine[:size], mine[size:]


def sum_chips(rows, half, me, parts, tensors, after, last):
    chips = parts // 2
    chip = me // 2
    rows = rows.reshape(chips, -1, rows.shape[1])
    rows, half = wait_for([rows, half], after)
    size = rows.shape[1]

    def of_chip(c):
        return jnp.concatenate([lax.dynamic_index_in_dim(rows, c, 0, keepdims=False), half])

    others = [permute(of_chip(chip ^ e), 2 * e, parts) for e in range(1, chips)]
    summed = lax.dynamic_index_in_dim(rows, chip, 0, keepdims=False)
    for other in wait_for(others, []):
        summed, half = summed + other[:size], half + other[size:]
    summed, half = wait_for([summed, half], [last])
    d = 1
    while 2 * d < tensors:
        summed = summed + permute(summed, d, tensors, "tensor")
        d *= 2
    beside = permute(summed, d, tensors, "tensor") if d < tensors else jnp.zeros_like(summed)
    return [summed, beside], [half, permute(half, 1, parts)]


def unpack(pieces, rows, halves, me, parts, after):
    summed, beside, half, other = wait_for(list(rows) + list(halves), after)
    summed = summed + beside
    out, start = [], 0
    for p in pieces:
        size = p.size // parts // summed.shape[1]
        out.append(summed[start : start + size].reshape(-1, p.shape[1]))
        start += size
    first, second = jnp.where(me % 2 == 0, half, other), jnp.where(me % 2 == 0, other, half)
    return out, jnp.concatenate([first, second])


def sum_halves(term, me, parts, scale):
    core = me % 2
    half = term.shape[0] // 2
    term = term + permute(term, 1, parts)
    return lax.dynamic_slice_in_dim(term, core * half, half, 0) * scale


def send_halves(mine, parts, after):
    (mine,) = wait_for([mine], after)
    return [mine] + [permute(mine, 2 * e, parts) for e in range(1, parts // 2)]


def sum_all(halves, me, parts, after):
    halves = wait_for(halves, after)
    total = halves[0]
    for half in halves[1:]:
        total = total + half
    other = permute(total, 1, parts)
    return jnp.where(
        me % 2 == 0, jnp.concatenate([total, other]), jnp.concatenate([other, total])
    )


def body(parts, tensors, inputs, kernel, w_in, w_gate, w_out, factor_a, factor_b, cotangent):
    rows, chans = inputs.shape
    inner = factor_a.shape[0]
    blocks = rows // inner
    span = inner // parts
    me = lax.axis_index("tm").astype(jnp.int32)
    me1 = me[None]
    x3 = inputs.reshape(blocks, inner, chans)
    kn3 = kernel.reshape(blocks, inner, chans)
    ct3 = cotangent.reshape(blocks, inner, chans)
    factor_at = factor_a.T
    dist = distances(parts)
    partners = [(me ^ d)[None] for d in dist]

    spread = jnp.concatenate([p * blocks + jnp.arange(blocks, dtype=jnp.int32) for p in partners])
    fb = jnp.take(jnp.take(factor_b, spread, axis=0), spread, axis=1)

    received, window = [], 5
    gs_out = [grad_second_call(p, x3, ct3, w_gate, w_out, span, ()) for p in partners]
    gs_in = send(dist, gs_out, received, window, parts)
    tw_out = twisted_call(me1, x3, kn3, w_in, factor_at, dist, ())
    tw_in = send(dist, tw_out, received, window, parts)
    gt_out = grad_twisted_call(fb, gs_in)
    gt_in = send(dist, gt_out, received, window, parts)
    se_out, fb_term = second_call(fb.T, tw_in, gs_in)
    gk, gm, fa_term, gwi_term = grad_mixed_call(
        me1, x3, kn3, w_in, factor_at, factor_a, dist, gt_in
    )
    se_out = list(se_out)
    tail = 2 * (parts - 1) // 7
    se_out[-tail - 1 :] = wait_for(se_out[-tail - 1 :], [gwi_term])
    se_in = send(dist[:-tail], se_out[:-tail], received, window, parts)
    arrays, terms = (), ()
    late = parts - tail
    for i in range(late):
        *arrays, term = outputs_call(
            partners[i], x3, ct3, gm, se_in[i], w_in, w_gate, w_out, arrays, terms
        )
        terms = [term]
        if i == 0:
            early = terms
            place = jnp.asarray([dist.index(d) for d in range(parts)], jnp.int32)
            natural = place[me ^ jnp.arange(parts, dtype=jnp.int32)]
            back = (natural[:, None] * blocks + jnp.arange(blocks, dtype=jnp.int32)).reshape(-1)
            fb_term = jnp.take(jnp.take(fb_term, back, axis=0), back, axis=1)
            fa_term, fb_term, gwi_term = wait_for([fa_term, fb_term, gwi_term], early)
            token_scale = 1.0 / math.sqrt(N1 * N2)
            pieces = [fa_term / math.sqrt(N1 * D), fb_term / math.sqrt(N2 * D)]
            in_rows, in_half = sum_cores(
                pieces, gwi_term.reshape(-1, w_in.shape[1]) * token_scale, me, parts
            )
            last = wait_for(se_out[-tail:], se_in[1 : 1 + parts // 4] )
            se_in += [permute(a, d, parts) for a, d in zip(last, dist[-tail:])]
    middle = terms
    for i in range(late, parts):
        terms = outputs_call(
            partners[i], x3, ct3, gm, se_in[i], w_in, w_gate, w_out, None, terms
        )
    (gw_term,) = terms
    gw_half = sum_halves(gw_term, me, parts, token_scale)
    in_rows, in_halves = sum_chips(in_rows, in_half, me, parts, tensors, middle, gw_half)
    halves = send_halves(gw_half, parts, [])
    se_in[late:] = wait_for(se_in[late:], in_rows[:1])
    for i in range(late, parts):
        arrays = outputs_call(
            partners[i], x3, ct3, gm, se_in[i], w_in, w_gate, w_out, arrays, None
        )
    outputs, grad_inputs = arrays
    summed = sum_all(halves, me, parts, arrays)
    (fa_sum, fb_sum), summed_in = unpack(pieces, in_rows, in_halves, me, parts, arrays)
    summed_in = summed_in.reshape(w_in.shape)
    summed_gate, summed_out = jnp.split(summed, 2)
    return (
        outputs.reshape(rows, chans),
        grad_inputs.reshape(rows, chans),
        gk.reshape(rows, chans),
        summed_in,
        summed_gate,
        summed_out,
        fa_sum,
        fb_sum,
    )


def solution(mesh):
    return jax.shard_map(
        functools.partial(body, mesh.shape["tm"], mesh.shape["tensor"]),
        mesh=mesh,
        in_specs=(
            P("tm", "tensor"),
            P("tm", "tensor"),
            P("tensor", None, None),
            P("tensor", None, None),
            P("tensor", None, None),
            P(),
            P(),
            P("tm", "tensor"),
        ),
        out_specs=(
            P("tm", "tensor"),
            P("tm", "tensor"),
            P("tm", "tensor"),
            P("tensor", None, None),
            P("tensor", None, None),
            P("tensor", None, None),
            P("tm", None),
            P("tm", None),
        ),
        check_vma=False,
    )
```
